32 devices in a mesh: group: 2 (over y), inst: 16 (over z, x, core).
Axes of the slice: x: 2, y: 2, z: 4, core: 2. Of those that a mesh axis runs over, the one named last changes fastest.
Arguments:
- kv_pool: bfloat16 [384, 128, 2048], P(('group', 'inst')), parts along dimension 0, as said below
- page_table: int32 [128, 3], P(('group', 'inst')), parts along dimension 0, may hold values from 0 to 11, as said below
- lengths: int32 [128], P(('group', 'inst')), parts along dimension 0, may hold values from 1 to 384, as said below
- query: bfloat16 [2, 128, 8192], P(None, ('group', 'inst')), parts along dimension 1, as said below
- new_kv: bfloat16 [2, 128, 2048], P(None, ('group', 'inst')), parts along dimension 1, may hold values from -6 to 6
- moves: int32 [128], P(('group', 'inst')), parts along dimension 0, may hold values from 0 to 3, as said below
Outputs:
- attended: bfloat16 [2, 128, 8192], P(None, ('group', 'inst')), parts along dimension 1
- guest_attended: bfloat16 [96, 8192], P(('group', 'inst')), parts along dimension 0
- moved_pages: bfloat16 [288, 128, 2048], P(('group', 'inst')), parts along dimension 0
The draws below stay inside these ranges and needn't reach their ends.
There are 2 independent parts, one for each index of `group`. The reference program is written for one: setup_inputs(seed, part) draws one part's arguments, and reference() takes and returns one part's arrays. A program takes and returns all parts, laid end to end along the dimension named above; each array names one. Nothing has to cross between parts.
Inputs may be any that keep to these rules, and one draw needn't show every extreme that they name: `page_table`: within one instance, the 4 sessions' page-table rows together name each of its 12 slots once. `lengths`: some session holds the full 3 pages. `moves`: among the sessions of one instance each distance 1 to 3 occurs exactly once; the others are 0. `query`: query entries are of order one or up to some tens. `kv_pool`: cached entries are of order one.
All inputs are finite; a program needn't handle non-finite values.
Results may differ from the reference program's by a relative error of at most 0.0051.
Values may be sent and summed in bfloat16 or wider, within the bound.
No kernel may reach another device: no remote copies, remote signals or barrier semaphores. Data moves between devices by JAX's collectives and lax.ppermute only.
A program may use at most 64 MiB of HBM per device.

```python
import jax
import jax.numpy as jnp
from jax import lax

HQ = 64
KVH = 8
HD = 128
PAGE = 128
MAXP = 3
SES_DEV = 4
REACH = 3
STEPS = 2
GRP = 8
PAGES_DEV = 12
SESSIONS = 64
POOL = 192
N_INST = 16


def draw_kv_pool(key, part):
    key = jax.random.fold_in(key, 11)
    values = jax.random.normal(key, (POOL, PAGE, 2 * KVH * HD), jnp.float32)
    return values.astype(jnp.bfloat16)


def draw_query(key, part):
    key = jax.random.fold_in(key, 13)
    values = jax.random.normal(key, (STEPS, SESSIONS, HQ * HD), jnp.float32)
    return values.astype(jnp.bfloat16)


def draw_page_table(key, part):
    key = jax.random.fold_in(key, 17)
    inst_keys = jax.random.split(key, SESSIONS // SES_DEV)
    slots = jax.vmap(lambda inner: jax.random.permutation(inner, PAGES_DEV))(inst_keys)
    return slots.reshape(SESSIONS, MAXP).astype(jnp.int32)


def draw_lengths(key, part):
    key = jax.random.fold_in(key, 19)
    values = jax.random.randint(key, (SESSIONS,), 1, MAXP * PAGE + 1, jnp.int32)
    return values.at[0].set(MAXP * PAGE)


def draw_moves(key, part):
    key = jax.random.fold_in(key, 23)
    inst_keys = jax.random.split(key, SESSIONS // SES_DEV)

    def per_inst(inner):
        shuffled = jax.random.permutation(inner, SES_DEV)
        ranking = jnp.argsort(shuffled).astype(jnp.int32)
        return jnp.where(ranking < REACH, ranking + 1, 0).astype(jnp.int32)
    return jax.vmap(per_inst)(inst_keys).reshape(SESSIONS)


def block_scale(own_key, shape, pieces, least, high):
    gain = 1.0
    for axis_at, parts in pieces:
        draws = jax.random.uniform(jax.random.fold_in(jax.random.fold_in(own_key, 6), axis_at), (parts,), jnp.float32, least / len(pieces), high / len(pieces))
        gain = gain * jnp.repeat(jnp.exp(draws), shape[axis_at] // parts).reshape((-1,) + (1,) * (len(shape) - 1 - axis_at))
    return gain


def bell_draw(stream_key, dims, deviation, reach, cuts=(), kind=jnp.bfloat16):
    gain = block_scale(stream_key, dims, cuts, -0.22, 0.18) if cuts else 1.0
    values = jax.random.normal(stream_key, dims, jnp.float32) * deviation * gain
    return jnp.minimum(jnp.maximum(values, -reach), reach).astype(kind)


def setup_inputs(seed: int = 0, part: int = 0) -> dict:
    key_list = jax.random.split(jax.random.key(seed), 7)
    part_splits = jax.random.split(jax.random.fold_in(key_list[6], part), 7)
    kv_pool = draw_kv_pool(jax.random.fold_in(jax.random.fold_in(key_list[6], part), 71), part)
    page_table = draw_page_table(jax.random.fold_in(jax.random.fold_in(key_list[6], part), 71), part)
    lengths = draw_lengths(jax.random.fold_in(jax.random.fold_in(key_list[6], part), 71), part)
    query = draw_query(jax.random.fold_in(jax.random.fold_in(key_list[6], part), 71), part)
    new_kv = bell_draw(part_splits[4], (STEPS, SESSIONS, 2 * KVH * HD), 1.0, 6.0, ((1, 16),))
    moves = draw_moves(jax.random.fold_in(jax.random.fold_in(key_list[6], part), 71), part)
    return dict(kv_pool=kv_pool, page_table=page_table, lengths=lengths, query=query, new_kv=new_kv, moves=moves)


def attend_one(cached, visible, query_row, fresh_row):
    flat_rows = cached.reshape(-1, 2, KVH, HD).astype(jnp.float32)
    key_rows = flat_rows[:, 0]
    value_rows = flat_rows[:, 1]
    query_heads = query_row.reshape(KVH, GRP, HD).astype(jnp.float32)
    fresh = fresh_row.reshape(2, KVH, HD).astype(jnp.float32)
    scale = 1.0 / jnp.sqrt(jnp.float32(HD))
    scores = jnp.einsum('kgd,tkd->kgt', query_heads, key_rows) * scale
    own_score = jnp.einsum('kgd,kd->kg', query_heads, fresh[0]) * scale
    scores = jnp.where(visible[None, None, :], scores, jnp.float32(-1e+30))
    highest = jnp.maximum(lax.optimization_barrier(jnp.max(scores, axis=-1)), own_score)
    expo = jnp.exp(scores - highest[..., None])
    own_expo = jnp.exp(own_score - highest)
    denominator = lax.optimization_barrier(jnp.sum(expo, axis=-1)) + own_expo
    weights = (expo / denominator[..., None]).astype(jnp.bfloat16).astype(jnp.float32)
    own_weight = (own_expo / denominator).astype(jnp.bfloat16).astype(jnp.float32)
    result = jnp.einsum('kgt,tkd->kgd', weights, value_rows)
    result = result + own_weight[..., None] * fresh[1][:, None, :]
    return result.reshape(HQ * HD).astype(jnp.bfloat16)

def reference(kv_pool, page_table, lengths, query, new_kv, moves):
    owner_inst = jnp.arange(SESSIONS, dtype=jnp.int32) // SES_DEV
    global_pages = owner_inst[:, None] * PAGES_DEV + page_table
    positions = jnp.arange(MAXP * PAGE, dtype=jnp.int32)

    def per_session(session):
        cached = kv_pool[global_pages[session]]
        visible = positions < lengths[session]
        outputs = [attend_one(cached, visible, query[step, session], new_kv[step, session]) for step in range(STEPS)]
        return jnp.stack(outputs)
    full = lax.map(per_session, jnp.arange(SESSIONS, dtype=jnp.int32))
    full = jnp.transpose(full, (1, 0, 2))
    ordering = jnp.argsort(moves.reshape(N_INST, SES_DEV), axis=1, stable=True).astype(jnp.int32)
    movers = jnp.arange(N_INST, dtype=jnp.int32)[:, None] * SES_DEV + ordering[:, SES_DEV - REACH:]
    dest = jnp.arange(N_INST, dtype=jnp.int32)[:, None]
    offsets = jnp.arange(1, REACH + 1, dtype=jnp.int32)[None, :]
    source = (dest - offsets) % N_INST
    arriving = movers[source, offsets - 1]
    moved_pages = kv_pool[global_pages[arriving]]
    guest_attended = full[1][arriving.reshape(-1)]
    second = jnp.where((moves > 0)[:, None], jnp.zeros_like(full[1]), full[1])
    attended = jnp.stack([full[0], second])
    return (attended, guest_attended, moved_pages.reshape(N_INST * REACH * MAXP, PAGE, 2 * KVH * HD))
```

```python
import functools

import jax
import jax.numpy as jnp
from jax import lax
from jax.experimental import pallas as pl
from jax.experimental.pallas import tpu as pltpu
from jax.sharding import PartitionSpec as P

HQ = 64
KVH = 8
HD = 128
REACH = 3
GRP = 8
STEPS = 2


def send(value, pairs):
    return lax.ppermute(value, "inst", pairs)


def shift_pairs(count, steps):
    return [(source, (source + steps) % count) for source in range(count)]


def relay_pairs(count):
    first = [(i, i - 3 if i % 4 == 3 else i + 1) for i in range(count)]
    second = [(i, (i + 4) % count if i % 4 == 0 else i) for i in range(count)]
    return first, second


def pack_kernel(moves_ref, table_ref, pool_ref, *refs):
    outs, sems = refs[:REACH], refs[REACH]
    copies = []
    for offset in range(1, REACH + 1):
        mover = jnp.int32(0)
        for session in range(1, table_ref.shape[0]):
            mover = jnp.where(moves_ref[session] == offset, jnp.int32(session), mover)
        for page in range(table_ref.shape[1]):
            copies.append(
                pltpu.make_async_copy(
                    pool_ref.at[table_ref[mover, page]],
                    outs[offset - 1].at[page],
                    sems.at[offset - 1, page],
                )
            )
            copies[-1].start()
    for copy in copies:
        copy.wait()


def pack(moves, page_table, kv_pool):
    pages = page_table.shape[1]
    piece = jax.ShapeDtypeStruct((pages,) + kv_pool.shape[1:], kv_pool.dtype)
    return pl.pallas_call(
        pack_kernel,
        out_shape=(piece,) * REACH,
        in_specs=[
            pl.BlockSpec(memory_space=pltpu.SMEM),
            pl.BlockSpec(memory_space=pltpu.SMEM),
            pl.BlockSpec(memory_space=pl.ANY),
        ],
        out_specs=(pl.BlockSpec(memory_space=pl.ANY),) * REACH,
        scratch_shapes=[pltpu.SemaphoreType.DMA((REACH, pages))],
        name="pack",
    )(moves, page_table, kv_pool)


def place_kernel(row, piece_ref, *refs):
    out_ref, sem = refs[-2], refs[-1]
    copy = pltpu.make_async_copy(piece_ref, out_ref.at[pl.ds(row, piece_ref.shape[0])], sem)
    copy.start()
    copy.wait()


def place(piece, row, total, buffer=None):
    args = (piece,) if buffer is None else (piece, buffer)
    return pl.pallas_call(
        functools.partial(place_kernel, row),
        out_shape=jax.ShapeDtypeStruct((total,) + piece.shape[1:], piece.dtype),
        in_specs=[pl.BlockSpec(memory_space=pl.ANY)] * len(args),
        out_specs=pl.BlockSpec(memory_space=pl.ANY),
        scratch_shapes=[pltpu.SemaphoreType.DMA],
        input_output_aliases={} if buffer is None else {1: 0},
        name="place",
    )(*args)


def attend_kernel(table_ref, lengths_ref, q_ref, nk_ref, nv_ref, *refs):
    page_refs, out_ref = refs[:-1], refs[-1]
    session = pl.program_id(0)
    length = lengths_ref[session]
    rows = page_refs[0].shape[1]
    half = KVH * HD
    scale = 1.0 / jnp.sqrt(jnp.float32(HD))
    spots = lax.broadcasted_iota(jnp.int32, (1, rows * len(page_refs)), 1)
    visible = spots < length
    for head in range(KVH):
        lanes = pl.ds(head * HD, HD)
        value_lanes = pl.ds(half + head * HD, HD)
        query = q_ref[0, head]
        scores = jnp.concatenate(
            [
                lax.dot_general(
                    query,
                    page[0, :, lanes],
                    (((1,), (1,)), ((), ())),
                    preferred_element_type=jnp.float32,
                )
                for page in page_refs
            ],
            axis=1,
        )
        scores = jnp.where(visible, scores * scale, jnp.float32(-1e30))
        own = (
            jnp.sum(
                query.astype(jnp.float32) * nk_ref[0, head].astype(jnp.float32),
                axis=1,
                keepdims=True,
            )
            * scale
        )
        highest = jnp.maximum(jnp.max(scores, axis=1, keepdims=True), own)
        expo = jnp.exp(scores - highest)
        own_expo = jnp.exp(own - highest)
        denominator = jnp.sum(expo, axis=1, keepdims=True) + own_expo
        weights = (expo / denominator).astype(jnp.bfloat16)
        own_weight = (own_expo / denominator).astype(jnp.bfloat16).astype(jnp.float32)
        result = own_weight * nv_ref[0, head].astype(jnp.float32)
        for at, page in enumerate(page_refs):
            result = result + jnp.dot(
                weights[:, at * rows : (at + 1) * rows],
                page[0, :, value_lanes],
                preferred_element_type=jnp.float32,
            )
        out_ref[0, head] = result.astype(jnp.bfloat16)


def attend(kv_pool, page_table, lengths, query, new_kv):
    sessions, pages = page_table.shape
    rows = STEPS * GRP
    queries = query.reshape(STEPS, sessions, KVH, GRP, HD).transpose(1, 2, 0, 3, 4)
    queries = queries.reshape(sessions, KVH, rows, HD)
    fresh = new_kv.reshape(STEPS, sessions, 2, KVH, 1, HD).transpose(2, 1, 3, 0, 4, 5)
    fresh = jnp.broadcast_to(fresh, (2, sessions, KVH, STEPS, GRP, HD))
    fresh = fresh.reshape(2, sessions, KVH, rows, HD)
    small = pl.BlockSpec((1, KVH, rows, HD), lambda s, table, lens: (s, 0, 0, 0))
    page_specs = [
        pl.BlockSpec((1,) + kv_pool.shape[1:], lambda s, table, lens, k=k: (table[s, k], 0, 0))
        for k in range(pages)
    ]
    return pl.pallas_call(
        attend_kernel,
        out_shape=jax.ShapeDtypeStruct((sessions, KVH, rows, HD), jnp.bfloat16),
        grid_spec=pltpu.PrefetchScalarGridSpec(
            num_scalar_prefetch=2,
            grid=(sessions,),
            in_specs=[small, small, small] + page_specs,
            out_specs=small,
        ),
        compiler_params=pltpu.CompilerParams(vmem_limit_bytes=24 << 20),
        cost_estimate=pl.CostEstimate(
            flops=4 * sessions * KVH * rows * HD * pages * 128,
            bytes_accessed=sessions * pages * 128 * 2048 * 2,
            transcendentals=sessions * KVH * rows * pages * 128,
        ),
        name="attend",
    )(page_table, lengths, queries, fresh[0], fresh[1], *([kv_pool] * pages))


def body(kv_pool, page_table, lengths, query, new_kv, moves):
    count = lax.axis_size("inst")
    sessions, pages = page_table.shape
    total = REACH * pages
    packed = pack(moves, page_table, kv_pool)
    query, new_kv, *packed = lax.optimization_barrier((query, new_kv, *packed))
    if count % 4 == 0:
        hops = relay_pairs(count)
    else:
        hops = (shift_pairs(count, 1),)
    near = send(packed[0], hops[0])
    far = send(packed[2], shift_pairs(count, 3))
    middle = send(packed[1], shift_pairs(count, 2))
    for hop in hops[1:]:
        near = send(near, hop)
    full = attend(kv_pool, page_table, lengths, query, new_kv)
    full = full.reshape(sessions, KVH, STEPS, GRP, HD).transpose(2, 0, 1, 3, 4)
    full = full.reshape(STEPS, sessions, HQ * HD)
    second = jnp.where((moves > 0)[:, None], jnp.zeros_like(full[1]), full[1])
    attended = jnp.stack([full[0], second])
    guests = []
    for offset in range(1, REACH + 1):
        leaving = jnp.argmax(moves == offset)
        row = lax.dynamic_slice_in_dim(full[1], leaving, 1, axis=0)
        guests.append(send(row, shift_pairs(count, offset)))
    guest_attended = jnp.concatenate(guests, axis=0)
    moved = place(far, 2 * pages, total)
    moved = place(near, 0, total, moved)
    moved = place(middle, pages, total, moved)
    return attended, guest_attended, moved


def solution(mesh):
    return jax.shard_map(
        body,
        mesh=mesh,
        in_specs=(
            P(("group", "inst"), None, None),
            P(("group", "inst"), None),
            P(("group", "inst")),
            P(None, ("group", "inst"), None),
            P(None, ("group", "inst"), None),
            P(("group", "inst")),
        ),
        out_specs=(
            P(None, ("group", "inst"), None),
            P(("group", "inst"), None),
            P(("group", "inst"), None, None),
        ),
        check_vma=False,
    )
```

```python
import functools

import jax
import jax.numpy as jnp
from jax import lax
from jax.experimental import pallas as pl
from jax.experimental.pallas import tpu as pltpu
from jax.sharding import PartitionSpec as P

HQ = 64
KVH = 8
HD = 128
REACH = 3
GRP = 8
STEPS = 2
SMALL = pl.CostEstimate(flops=0, bytes_accessed=0, transcendentals=0)
LITTLE = 4 << 20


def send(value, pairs):
    return lax.ppermute(value, "inst", pairs)


def shift_pairs(count, steps):
    return [(source, (source + steps) % count) for source in range(count)]


def relay_pairs(count):
    first = [(i, i - 3 if i % 4 == 3 else i + 1) for i in range(count)]
    second = [(i, (i + 4) % count if i % 4 == 0 else i) for i in range(count)]
    return first, second


def pack_kernel(offsets, moves_ref, table_ref, pool_ref, *refs):
    outs, held, in_sems, out_sems = refs[: len(offsets)], *refs[-3:]
    spots, reads, writes = [], [], []
    for at, offset in enumerate(offsets):
        mover = jnp.int32(0)
        for session in range(1, table_ref.shape[0]):
            mover = jnp.where(moves_ref[session] == offset, jnp.int32(session), mover)
        for page in range(table_ref.shape[1]):
            spots.append((at, page))
            reads.append(
                pltpu.make_async_copy(
                    pool_ref.at[table_ref[mover, page]], held.at[at, page], in_sems.at[at, page]
                )
            )
            reads[-1].start()
    for (at, page), read in zip(spots, reads):
        read.wait()
        writes.append(
            pltpu.make_async_copy(held.at[at, page], outs[at].at[page], out_sems.at[at, page])
        )
        writes[-1].start()
    for write in writes:
        write.wait()


def pack(offsets, moves, page_table, kv_pool):
    pages = page_table.shape[1]
    count = len(offsets)
    piece = jax.ShapeDtypeStruct((pages,) + kv_pool.shape[1:], kv_pool.dtype)
    return pl.pallas_call(
        functools.partial(pack_kernel, offsets),
        out_shape=(piece,) * count,
        in_specs=[
            pl.BlockSpec(memory_space=pltpu.SMEM),
            pl.BlockSpec(memory_space=pltpu.SMEM),
            pl.BlockSpec(memory_space=pltpu.HBM),
        ],
        out_specs=(pl.BlockSpec(memory_space=pl.ANY),) * count,
        scratch_shapes=[
            pltpu.VMEM((count, pages) + kv_pool.shape[1:], kv_pool.dtype),
            pltpu.SemaphoreType.DMA((count, pages)),
            pltpu.SemaphoreType.DMA((count, pages)),
        ],
        compiler_params=pltpu.CompilerParams(vmem_limit_bytes=8 << 20),
        cost_estimate=SMALL,
        name="pack",
    )(moves, page_table, pltpu.with_memory_space_constraint(kv_pool, pltpu.HBM))


def place_kernel(row, piece_ref, *refs):
    out_ref, sem = refs[-2], refs[-1]
    copy = pltpu.make_async_copy(piece_ref, out_ref.at[pl.ds(row, piece_ref.shape[0])], sem)
    copy.start()
    copy.wait()


def place(piece, row, total, buffer=None):
    args = (pltpu.with_memory_space_constraint(piece, pltpu.VMEM),)
    if buffer is not None:
        args += (buffer,)
    return pl.pallas_call(
        functools.partial(place_kernel, row),
        out_shape=pltpu.HBM((total,) + piece.shape[1:], piece.dtype),
        in_specs=[
            pl.BlockSpec(memory_space=pltpu.VMEM),
            pl.BlockSpec(memory_space=pltpu.HBM),
        ][: len(args)],
        out_specs=pl.BlockSpec(memory_space=pltpu.HBM),
        scratch_shapes=[pltpu.SemaphoreType.DMA],
        input_output_aliases={} if buffer is None else {1: 0},
        compiler_params=pltpu.CompilerParams(vmem_limit_bytes=LITTLE),
        cost_estimate=SMALL,
        name="place",
    )(*args)


def attend_kernel(table_ref, lengths_ref, moves_ref, q_ref, nk_ref, nv_ref, *refs):
    page_refs, out_ref, guest_ref = refs[:-2], refs[-2], refs[-1]
    session = pl.program_id(0)
    length = lengths_ref[session]
    move = moves_ref[session]
    rows = page_refs[0].shape[1]
    half = KVH * HD
    scale = 1.0 / jnp.sqrt(jnp.float32(HD))
    spots = lax.broadcasted_iota(jnp.int32, (1, rows * len(page_refs)), 1)
    visible = spots < length
    for head in range(KVH):
        lanes = pl.ds(head * HD, HD)
        value_lanes = pl.ds(half + head * HD, HD)
        query = q_ref[0, head]
        scores = jnp.concatenate(
            [
                lax.dot_general(
                    query,
                    page[0, :, lanes],
                    (((1,), (1,)), ((), ())),
                    preferred_element_type=jnp.float32,
                )
                for page in page_refs
            ],
            axis=1,
        )
        scores = jnp.where(visible, scores * scale, jnp.float32(-1e30))
        own = (
            jnp.sum(
                query.astype(jnp.float32) * nk_ref[0, head].astype(jnp.float32),
                axis=1,
                keepdims=True,
            )
            * scale
        )
        highest = jnp.maximum(jnp.max(scores, axis=1, keepdims=True), own)
        expo = jnp.exp(scores - highest)
        own_expo = jnp.exp(own - highest)
        denominator = jnp.sum(expo, axis=1, keepdims=True) + own_expo
        weights = (expo / denominator).astype(jnp.bfloat16)
        own_weight = (own_expo / denominator).astype(jnp.bfloat16).astype(jnp.float32)
        result = own_weight * nv_ref[0, head].astype(jnp.float32)
        for at, page in enumerate(page_refs):
            result = result + jnp.dot(
                weights[:, at * rows : (at + 1) * rows],
                page[0, :, value_lanes],
                preferred_element_type=jnp.float32,
            )
        result = result.astype(jnp.bfloat16)
        heads = pl.ds(head * GRP, GRP)
        later = result[GRP:]
        out_ref[0, 0, heads] = result[:GRP]
        out_ref[1, 0, heads] = jnp.where(move > 0, jnp.zeros_like(later), later)

        @pl.when(move > 0)
        def _():
            guest_ref[jnp.maximum(move - 1, 0), heads] = later


def attend(kv_pool, page_table, lengths, moves, query, new_kv):
    sessions, pages = page_table.shape
    rows = STEPS * GRP
    queries = query.reshape(STEPS, sessions, KVH, GRP, HD).transpose(1, 2, 0, 3, 4)
    queries = queries.reshape(sessions, KVH, rows, HD)
    fresh = new_kv.reshape(STEPS, sessions, 2, KVH, 1, HD).transpose(2, 1, 3, 0, 4, 5)
    fresh = jnp.broadcast_to(fresh, (2, sessions, KVH, STEPS, GRP, HD))
    fresh = fresh.reshape(2, sessions, KVH, rows, HD)
    small = pl.BlockSpec((1, KVH, rows, HD), lambda s, *_: (s, 0, 0, 0))
    page_specs = [
        pl.BlockSpec((1,) + kv_pool.shape[1:], lambda s, table, *_, k=k: (table[s, k], 0, 0))
        for k in range(pages)
    ]
    return pl.pallas_call(
        attend_kernel,
        out_shape=(
            jax.ShapeDtypeStruct((STEPS, sessions, HQ, HD), jnp.bfloat16),
            jax.ShapeDtypeStruct((REACH, HQ, HD), jnp.bfloat16),
        ),
        grid_spec=pltpu.PrefetchScalarGridSpec(
            num_scalar_prefetch=3,
            grid=(sessions,),
            in_specs=[small, small, small] + page_specs,
            out_specs=(
                pl.BlockSpec((STEPS, 1, HQ, HD), lambda s, *_: (0, s, 0, 0)),
                pl.BlockSpec((REACH, HQ, HD), lambda s, *_: (0, 0, 0)),
            ),
        ),
        compiler_params=pltpu.CompilerParams(vmem_limit_bytes=24 << 20),
        cost_estimate=SMALL,
        name="attend",
    )(page_table, lengths, moves, queries, fresh[0], fresh[1], *([pltpu.with_memory_space_constraint(kv_pool, pltpu.HBM)] * pages))


def body(kv_pool, page_table, lengths, query, new_kv, moves):
    count = lax.axis_size("inst")
    sessions, pages = page_table.shape
    total = REACH * pages
    near, far = pack((1, 3), moves, page_table, kv_pool)
    near, far, table, query, new_kv = lax.optimization_barrier(
        (near, far, page_table, query, new_kv)
    )
    (middle,) = pack((2,), moves, table, kv_pool)
    full, leaving = attend(kv_pool, table, lengths, moves, query, new_kv)
    full, leaving, middle = lax.optimization_barrier((full, leaving, middle))
    if count % 4 == 0:
        hops = relay_pairs(count)
    else:
        hops = (shift_pairs(count, 1),)
    near = send(near, hops[0])
    far = send(far, shift_pairs(count, 3))
    attended = full.reshape(STEPS, sessions, HQ * HD)
    leaving = leaving.reshape(REACH, HQ * HD)
    middle = send(middle, shift_pairs(count, 2))
    near, leaving = lax.optimization_barrier((near, leaving))
    guests = [
        send(leaving[offset - 1 : offset], shift_pairs(count, offset))
        for offset in range(1, REACH + 1)
    ]
    near, far = lax.optimization_barrier((near, far))
    for hop in hops[1:]:
        near = send(near, hop)
    guest_attended = jnp.concatenate(guests, axis=0)
    moved = place(far, 2 * pages, total)
    moved = place(near, 0, total, moved)
    moved = place(middle, pages, total, moved)
    return attended, guest_attended, moved


def solution(mesh):
    return jax.shard_map(
        body,
        mesh=mesh,
        in_specs=(
            P(("group", "inst"), None, None),
            P(("group", "inst"), None),
            P(("group", "inst")),
            P(None, ("group", "inst"), None),
            P(None, ("group", "inst"), None),
            P(("group", "inst")),
        ),
        out_specs=(
            P(None, ("group", "inst"), None),
            P(("group", "inst"), None),
            P(("group", "inst"), None, None),
        ),
        check_vma=False,
    )
```

```python
import functools

import jax
import jax.numpy as jnp
from jax import lax
from jax.experimental import pallas as pl
from jax.experimental.pallas import tpu as pltpu
from jax.sharding import PartitionSpec as P

HQ = 64
KVH = 8
HD = 128
REACH = 3
GRP = 8
STEPS = 2
SMALL = pl.CostEstimate(flops=0, bytes_accessed=0, transcendentals=0)
LITTLE = 5 << 20
PARTS = 2


def send(value, pairs):
    return lax.ppermute(value, "inst", pairs)


def shift_pairs(count, steps):
    return [(source, (source + steps) % count) for source in range(count)]


def relay_pairs(count):
    first = [(i, i - 3 if i % 4 == 3 else i + 1) for i in range(count)]
    second = [(i, (i + 4) % count if i % 4 == 0 else i) for i in range(count)]
    return first, second


def pack_kernel(offsets, moves_ref, table_ref, pool_ref, *refs):
    outs, held, in_sems, out_sems = refs[: len(offsets)], *refs[-3:]
    spots, reads, writes = [], [], []
    for at, offset in enumerate(offsets):
        mover = jnp.int32(0)
        for session in range(1, table_ref.shape[0]):
            mover = jnp.where(moves_ref[session] == offset, jnp.int32(session), mover)
        for page in range(table_ref.shape[1]):
            spots.append((at, page))
            reads.append(
                pltpu.make_async_copy(
                    pool_ref.at[table_ref[mover, page]], held.at[at, page], in_sems.at[at, page]
                )
            )
            reads[-1].start()
    for (at, page), read in zip(spots, reads):
        read.wait()
        writes.append(
            pltpu.make_async_copy(held.at[at, page], outs[at].at[page], out_sems.at[at, page])
        )
        writes[-1].start()
    for write in writes:
        write.wait()


def pack(offsets, moves, page_table, kv_pool):
    pages = page_table.shape[1]
    count = len(offsets)
    piece = jax.ShapeDtypeStruct((pages,) + kv_pool.shape[1:], kv_pool.dtype)
    return pl.pallas_call(
        functools.partial(pack_kernel, offsets),
        out_shape=(piece,) * count,
        in_specs=[
            pl.BlockSpec(memory_space=pltpu.SMEM),
            pl.BlockSpec(memory_space=pltpu.SMEM),
            pl.BlockSpec(memory_space=pltpu.HBM),
        ],
        out_specs=(pl.BlockSpec(memory_space=pl.ANY),) * count,
        scratch_shapes=[
            pltpu.VMEM((count, pages) + kv_pool.shape[1:], kv_pool.dtype),
            pltpu.SemaphoreType.DMA((count, pages)),
            pltpu.SemaphoreType.DMA((count, pages)),
        ],
        compiler_params=pltpu.CompilerParams(vmem_limit_bytes=LITTLE),
        cost_estimate=SMALL,
        name="pack",
    )(*(pltpu.with_memory_space_constraint(x, pltpu.HBM) for x in (moves, page_table, kv_pool)))


def place_kernel(row, guests, piece_ref, *refs):
    guest_refs, refs = refs[:guests], refs[guests:]
    held, in_sems, out_sems = refs[-3:]
    out_ref = refs[-5] if guests else refs[-4]
    rows = piece_ref.shape[1] // PARTS
    reads, writes = [], []
    for page in range(piece_ref.shape[0]):
        for part in range(PARTS):
            lines = pl.ds(part * rows, rows)
            reads.append(
                pltpu.make_async_copy(
                    piece_ref.at[page, lines], held.at[page, lines], in_sems.at[page, part]
                )
            )
            writes.append(
                pltpu.make_async_copy(
                    held.at[page, lines], out_ref.at[row + page, lines], out_sems.at[page, part]
                )
            )
            reads[-1].start()
    if guests:
        refs[-4][...] = jnp.concatenate([guest[...] for guest in guest_refs], axis=0)
    for read, write in zip(reads, writes):
        read.wait()
        write.start()
    for write in writes:
        write.wait()


def place(piece, row, total, buffer=None, guests=()):
    args = (piece, *guests)
    aliases = {}
    if buffer is not None:
        aliases = {len(args): 0}
        args += (buffer,)
    shapes = [pltpu.HBM((total,) + piece.shape[1:], piece.dtype)]
    specs = [pl.BlockSpec(memory_space=pltpu.HBM)]
    if guests:
        shapes.append(jax.ShapeDtypeStruct((len(guests), guests[0].shape[1]), guests[0].dtype))
        specs.append(pl.BlockSpec(memory_space=pltpu.VMEM))
    return pl.pallas_call(
        functools.partial(place_kernel, row, len(guests)),
        out_shape=tuple(shapes),
        in_specs=[pl.BlockSpec(memory_space=pl.ANY)]
        + [pl.BlockSpec(memory_space=pltpu.VMEM)] * len(guests)
        + [pl.BlockSpec(memory_space=pltpu.HBM)] * len(aliases),
        out_specs=tuple(specs),
        scratch_shapes=[
            pltpu.VMEM(piece.shape, piece.dtype),
            pltpu.SemaphoreType.DMA((piece.shape[0], PARTS)),
            pltpu.SemaphoreType.DMA((piece.shape[0], PARTS)),
        ],
        input_output_aliases=aliases,
        compiler_params=pltpu.CompilerParams(vmem_limit_bytes=LITTLE),
        cost_estimate=SMALL,
        name="place",
    )(*args)


def attend_kernel(moves_ref, table_ref, lengths_ref, pool_ref, query_ref, fresh_ref, *refs):
    out_ref, guest_refs = refs[0], refs[1 : 1 + REACH]
    held, asked, answered, sems = refs[1 + REACH :]
    sessions, pages = table_ref.shape
    span = pages * held.shape[2]
    reads = []
    for session in range(sessions):
        for page in range(pages):
            reads.append(
                pltpu.make_async_copy(
                    pool_ref.at[table_ref[session, page]],
                    held.at[session, page],
                    sems.at[session, page],
                )
            )
            reads[-1].start()
    for head in range(HQ):
        lanes = pl.ds(head * HD, HD)
        for step in range(STEPS):
            asked[head, pl.ds(step * sessions, sessions)] = query_ref[step, :, lanes].astype(
                jnp.float32
            )
    scale = 1.0 / jnp.sqrt(jnp.float32(HD))
    spots = lax.broadcasted_iota(jnp.int32, (1, span), 1)
    for session in range(sessions):
        for page in range(pages):
            reads[session * pages + page].wait()
        visible = spots < lengths_ref[session]
        for head in range(KVH):
            heads = pl.ds(head * GRP, GRP)
            keys = held[session, :, :, pl.ds(head * HD, HD)].reshape(span, HD)
            values = held[session, :, :, pl.ds((KVH + head) * HD, HD)].reshape(span, HD)
            query = jnp.concatenate(
                [asked[heads, step * sessions + session, :] for step in range(STEPS)], axis=0
            )

            def spread(first):
                rows = [
                    fresh_ref[step, :, pl.ds(first, HD)].astype(jnp.float32)[session : session + 1]
                    for step in range(STEPS)
                ]
                return jnp.concatenate([jnp.broadcast_to(row, (GRP, HD)) for row in rows], axis=0)

            scores = lax.dot_general(
                query.astype(jnp.bfloat16),
                keys,
                (((1,), (1,)), ((), ())),
                preferred_element_type=jnp.float32,
            )
            scores = jnp.where(visible, scores * scale, jnp.float32(-1e30))
            own = jnp.sum(query * spread(head * HD), axis=1, keepdims=True) * scale
            highest = jnp.maximum(jnp.max(scores, axis=1, keepdims=True), own)
            expo = jnp.exp(scores - highest)
            own_expo = jnp.exp(own - highest)
            denominator = jnp.sum(expo, axis=1, keepdims=True) + own_expo
            weights = (expo / denominator).astype(jnp.bfloat16)
            own_weight = (own_expo / denominator).astype(jnp.bfloat16).astype(jnp.float32)
            result = jnp.dot(weights, values, preferred_element_type=jnp.float32)
            result = result + own_weight * spread((KVH + head) * HD)
            for step in range(STEPS):
                answered[heads, step * sessions + session, :] = result[
                    step * GRP : (step + 1) * GRP
                ]
    rows = lax.broadcasted_iota(jnp.int32, (sessions, HD), 0)
    distance = jnp.zeros((sessions, HD), jnp.int32)
    for session in range(sessions):
        distance = jnp.where(rows == session, moves_ref[session], distance)
    for head in range(HQ):
        lanes = pl.ds(head * HD, HD)
        first = answered[head, pl.ds(0, sessions)]
        second = answered[head, pl.ds(sessions, sessions)]
        out_ref[0, :, lanes] = first.astype(jnp.bfloat16)
        out_ref[1, :, lanes] = jnp.where(distance > 0, 0.0, second).astype(jnp.bfloat16)
        for offset in range(1, REACH + 1):
            row = jnp.sum(jnp.where(distance == offset, second, 0.0), axis=0, keepdims=True)
            guest_refs[offset - 1][:, lanes] = row.astype(jnp.bfloat16)


def attend(kv_pool, page_table, lengths, moves, query, new_kv):
    sessions, pages = page_table.shape
    guest = jax.ShapeDtypeStruct((1, query.shape[2]), query.dtype)
    return pl.pallas_call(
        attend_kernel,
        out_shape=(jax.ShapeDtypeStruct(query.shape, query.dtype),) + (guest,) * REACH,
        in_specs=[pl.BlockSpec(memory_space=pltpu.SMEM)] * 3
        + [pl.BlockSpec(memory_space=pltpu.HBM)]
        + [pl.BlockSpec(memory_space=pltpu.VMEM)] * 2,
        out_specs=(pl.BlockSpec(memory_space=pltpu.VMEM),) * (1 + REACH),
        scratch_shapes=[
            pltpu.VMEM((sessions, pages) + kv_pool.shape[1:], kv_pool.dtype),
            pltpu.VMEM((HQ, STEPS * sessions, HD), jnp.float32),
            pltpu.VMEM((HQ, STEPS * sessions, HD), jnp.float32),
            pltpu.SemaphoreType.DMA((sessions, pages)),
        ],
        compiler_params=pltpu.CompilerParams(vmem_limit_bytes=16 << 20),
        cost_estimate=SMALL,
        name="attend",
    )(
        *(
            pltpu.with_memory_space_constraint(x, pltpu.HBM)
            for x in (moves, page_table, lengths, kv_pool, query, new_kv)
        )
    )


def body(kv_pool, page_table, lengths, query, new_kv, moves):
    count = lax.axis_size("inst")
    sessions, pages = page_table.shape
    total = REACH * pages
    near, far = pack((1, 3), moves, page_table, kv_pool)
    near, far, table, query, new_kv = lax.optimization_barrier(
        (near, far, page_table, query, new_kv)
    )
    (middle,) = pack((2,), moves, table, kv_pool)
    attended, *leaving = attend(kv_pool, table, lengths, moves, query, new_kv)
    attended, middle, *leaving = lax.optimization_barrier((attended, middle, *leaving))
    if count % 4 == 0:
        hops = relay_pairs(count)
    else:
        hops = (shift_pairs(count, 1),)
    near = send(near, hops[0])
    far = send(far, shift_pairs(count, 3))
    middle = send(middle, shift_pairs(count, 2))
    guests = [
        send(leaving[offset - 1], shift_pairs(count, offset))
        for offset in range(1, REACH + 1)
    ]
    for hop in hops[1:]:
        near = send(near, hop)
    (moved,) = place(far, 2 * pages, total)
    (moved,) = place(middle, pages, total, moved)
    moved, near, *guests = lax.optimization_barrier((moved, near, *guests))
    moved, guest_attended = place(near, 0, total, moved, guests)
    return attended, guest_attended, moved


def solution(mesh):
    return jax.shard_map(
        body,
        mesh=mesh,
        in_specs=(
            P(("group", "inst"), None, None),
            P(("group", "inst"), None),
            P(("group", "inst")),
            P(None, ("group", "inst"), None),
            P(None, ("group", "inst"), None),
            P(("group", "inst")),
        ),
        out_specs=(
            P(None, ("group", "inst"), None),
            P(("group", "inst"), None),
            P(("group", "inst"), None, None),
        ),
        check_vma=False,
    )
```

```python
import functools

import jax
import jax.numpy as jnp
from jax import lax
from jax.experimental import pallas as pl
from jax.experimental.pallas import tpu as pltpu
from jax.sharding import PartitionSpec as P

HQ = 64
KVH = 8
HD = 128
REACH = 3
GRP = 8
STEPS = 2
SMALL = pl.CostEstimate(flops=0, bytes_accessed=0, transcendentals=0)
LITTLE = 1 << 20


def send(value, pairs):
    return lax.ppermute(value, "inst", pairs)


def shift_pairs(count, steps):
    return [(source, (source + steps) % count) for source in range(count)]


def relay_pairs(count):
    first = [(i, i - 3 if i % 4 == 3 else i + 1) for i in range(count)]
    second = [(i, (i + 4) % count if i % 4 == 0 else i) for i in range(count)]
    return first, second


def pack_kernel(offsets, moves_ref, table_ref, pool_ref, *refs):
    outs, sems = refs[:-1], refs[-1]
    copies = []
    for at, offset in enumerate(offsets):
        mover = jnp.int32(0)
        for session in range(1, table_ref.shape[0]):
            mover = jnp.where(moves_ref[session] == offset, jnp.int32(session), mover)
        for page in range(table_ref.shape[1]):
            copies.append(
                pltpu.make_async_copy(
                    pool_ref.at[table_ref[mover, page]], outs[at].at[page], sems.at[at, page]
                )
            )
            copies[-1].start()
    for copy in copies:
        copy.wait()


def pack(offsets, moves, page_table, kv_pool):
    pages = page_table.shape[1]
    piece = jax.ShapeDtypeStruct((pages,) + kv_pool.shape[1:], kv_pool.dtype)
    return pl.pallas_call(
        functools.partial(pack_kernel, offsets),
        out_shape=(piece,) * len(offsets),
        in_specs=[
            pl.BlockSpec(memory_space=pltpu.SMEM),
            pl.BlockSpec(memory_space=pltpu.SMEM),
            pl.BlockSpec(memory_space=pltpu.HBM),
        ],
        out_specs=(pl.BlockSpec(memory_space=pl.ANY),) * len(offsets),
        scratch_shapes=[pltpu.SemaphoreType.DMA((len(offsets), pages))],
        compiler_params=pltpu.CompilerParams(vmem_limit_bytes=LITTLE),
        cost_estimate=SMALL,
        name="pack",
    )(*(pltpu.with_memory_space_constraint(x, pltpu.HBM) for x in (moves, page_table, kv_pool)))


def place_kernel(rows, guests, *refs):
    pieces, refs = refs[: len(rows)], refs[len(rows) :]
    guest_refs, refs = refs[:guests], refs[guests:]
    if guests:
        out_ref, guest_out_ref, held, sem, guest_sem = refs[-5:]
    else:
        out_ref, sem = refs[-2:]
    copies = []
    for at, (row, piece) in enumerate(zip(rows, pieces)):
        copies.append(
            pltpu.make_async_copy(piece, out_ref.at[pl.ds(row, piece.shape[0])], sem.at[at])
        )
        copies[-1].start()
    if guests:
        held[...] = jnp.concatenate([guest[...] for guest in guest_refs], axis=0)
        copies.append(pltpu.make_async_copy(held, guest_out_ref, guest_sem))
        copies[-1].start()
    for copy in copies:
        copy.wait()


def place(pieces, rows, total, buffer=None, guests=()):
    args = (*pieces, *guests)
    aliases = {}
    if buffer is not None:
        aliases = {len(args): 0}
        args += (buffer,)
    shapes = [pltpu.HBM((total,) + pieces[0].shape[1:], pieces[0].dtype)]
    scratch = [pltpu.SemaphoreType.DMA((len(pieces),))]
    if guests:
        guest = (len(guests), guests[0].shape[1])
        shapes.append(pltpu.HBM(guest, guests[0].dtype))
        scratch = [pltpu.VMEM(guest, guests[0].dtype)] + scratch + [pltpu.SemaphoreType.DMA]
    return pl.pallas_call(
        functools.partial(place_kernel, rows, len(guests)),
        out_shape=tuple(shapes),
        in_specs=[pl.BlockSpec(memory_space=pl.ANY)] * len(pieces)
        + [pl.BlockSpec(memory_space=pltpu.VMEM)] * len(guests)
        + [pl.BlockSpec(memory_space=pltpu.HBM)] * len(aliases),
        out_specs=(pl.BlockSpec(memory_space=pltpu.HBM),) * len(shapes),
        scratch_shapes=scratch,
        input_output_aliases=aliases,
        compiler_params=pltpu.CompilerParams(vmem_limit_bytes=LITTLE),
        cost_estimate=SMALL,
        name="place",
    )(*args)


def attend_kernel(moves_ref, table_ref, lengths_ref, pool_ref, query_ref, fresh_ref, *refs):
    out_ref, guest_refs = refs[0], refs[1 : 1 + REACH]
    held, asked, answered, sems = refs[1 + REACH :]
    sessions, pages = table_ref.shape
    span = pages * held.shape[2]
    reads = []
    for session in range(sessions):
        for page in range(pages):
            reads.append(
                pltpu.make_async_copy(
                    pool_ref.at[table_ref[session, page]],
                    held.at[session, page],
                    sems.at[session, page],
                )
            )
            reads[-1].start()
    for head in range(HQ):
        lanes = pl.ds(head * HD, HD)
        for step in range(STEPS):
            asked[head, pl.ds(step * sessions, sessions)] = query_ref[step, :, lanes].astype(
                jnp.float32
            )
    scale = 1.0 / jnp.sqrt(jnp.float32(HD))
    spots = lax.broadcasted_iota(jnp.int32, (1, span), 1)
    for session in range(sessions):
        for page in range(pages):
            reads[session * pages + page].wait()
        visible = spots < lengths_ref[session]
        for head in range(KVH):
            heads = pl.ds(head * GRP, GRP)
            keys = held[session, :, :, pl.ds(head * HD, HD)].reshape(span, HD)
            values = held[session, :, :, pl.ds((KVH + head) * HD, HD)].reshape(span, HD)
            query = jnp.concatenate(
                [asked[heads, step * sessions + session, :] for step in range(STEPS)], axis=0
            )

            def spread(first):
                rows = [
                    fresh_ref[step, :, pl.ds(first, HD)].astype(jnp.float32)[session : session + 1]
                    for step in range(STEPS)
                ]
                return jnp.concatenate([jnp.broadcast_to(row, (GRP, HD)) for row in rows], axis=0)

            scores = lax.dot_general(
                query.astype(jnp.bfloat16),
                keys,
                (((1,), (1,)), ((), ())),
                preferred_element_type=jnp.float32,
            )
            scores = jnp.where(visible, scores * scale, jnp.float32(-1e30))
            own = jnp.sum(query * spread(head * HD), axis=1, keepdims=True) * scale
            highest = jnp.maximum(jnp.max(scores, axis=1, keepdims=True), own)
            expo = jnp.exp(scores - highest)
            own_expo = jnp.exp(own - highest)
            denominator = jnp.sum(expo, axis=1, keepdims=True) + own_expo
            weights = (expo / denominator).astype(jnp.bfloat16)
            own_weight = (own_expo / denominator).astype(jnp.bfloat16).astype(jnp.float32)
            result = jnp.dot(weights, values, preferred_element_type=jnp.float32)
            result = result + own_weight * spread((KVH + head) * HD)
            for step in range(STEPS):
                answered[heads, step * sessions + session, :] = result[
                    step * GRP : (step + 1) * GRP
                ]
    rows = lax.broadcasted_iota(jnp.int32, (sessions, HD), 0)
    distance = jnp.zeros((sessions, HD), jnp.int32)
    for session in range(sessions):
        distance = jnp.where(rows == session, moves_ref[session], distance)
    for head in range(HQ):
        lanes = pl.ds(head * HD, HD)
        first = answered[head, pl.ds(0, sessions)]
        second = answered[head, pl.ds(sessions, sessions)]
        out_ref[0, :, lanes] = first.astype(jnp.bfloat16)
        out_ref[1, :, lanes] = jnp.where(distance > 0, 0.0, second).astype(jnp.bfloat16)
        for offset in range(1, REACH + 1):
            row = jnp.sum(jnp.where(distance == offset, second, 0.0), axis=0, keepdims=True)
            guest_refs[offset - 1][:, lanes] = row.astype(jnp.bfloat16)


def attend(kv_pool, page_table, lengths, moves, query, new_kv):
    sessions, pages = page_table.shape
    guest = jax.ShapeDtypeStruct((1, query.shape[2]), query.dtype)
    return pl.pallas_call(
        attend_kernel,
        out_shape=(jax.ShapeDtypeStruct(query.shape, query.dtype),) + (guest,) * REACH,
        in_specs=[pl.BlockSpec(memory_space=pltpu.SMEM)] * 3
        + [pl.BlockSpec(memory_space=pltpu.HBM)]
        + [pl.BlockSpec(memory_space=pltpu.VMEM)] * 2,
        out_specs=(pl.BlockSpec(memory_space=pltpu.VMEM),) * (1 + REACH),
        scratch_shapes=[
            pltpu.VMEM((sessions, pages) + kv_pool.shape[1:], kv_pool.dtype),
            pltpu.VMEM((HQ, STEPS * sessions, HD), jnp.float32),
            pltpu.VMEM((HQ, STEPS * sessions, HD), jnp.float32),
            pltpu.SemaphoreType.DMA((sessions, pages)),
        ],
        compiler_params=pltpu.CompilerParams(vmem_limit_bytes=16 << 20),
        cost_estimate=SMALL,
        name="attend",
    )(
        *(
            pltpu.with_memory_space_constraint(x, pltpu.HBM)
            for x in (moves, page_table, lengths, kv_pool, query, new_kv)
        )
    )


def body(kv_pool, page_table, lengths, query, new_kv, moves):
    count = lax.axis_size("inst")
    sessions, pages = page_table.shape
    total = REACH * pages
    near, far = pack((1, 3), moves, page_table, kv_pool)
    near, far, table, query, new_kv = lax.optimization_barrier(
        (near, far, page_table, query, new_kv)
    )
    (middle,) = pack((2,), moves, table, kv_pool)
    attended, *leaving = attend(kv_pool, table, lengths, moves, query, new_kv)
    attended, middle, *leaving = lax.optimization_barrier((attended, middle, *leaving))
    if count % 4 == 0:
        hops = relay_pairs(count)
    else:
        hops = (shift_pairs(count, 1),)
    near = send(near, hops[0])
    far = send(far, shift_pairs(count, 3))
    middle = send(middle, shift_pairs(count, 2))
    guests = [
        send(leaving[offset - 1], shift_pairs(count, offset))
        for offset in range(1, REACH + 1)
    ]
    (moved,) = place((far,), (2 * pages,), total)
    near, moved = lax.optimization_barrier((near, moved))
    for hop in hops[1:]:
        near = send(near, hop)
    moved, guest_attended = place((middle, near), (pages, 0), total, moved, guests)
    return attended, guest_attended, moved


def solution(mesh):
    return jax.shard_map(
        body,
        mesh=mesh,
        in_specs=(
            P(("group", "inst"), None, None),
            P(("group", "inst"), None),
            P(("group", "inst")),
            P(None, ("group", "inst"), None),
            P(None, ("group", "inst"), None),
            P(("group", "inst")),
        ),
        out_specs=(
            P(None, ("group", "inst"), None),
            P(("group", "inst"), None),
            P(("group", "inst"), None, None),
        ),
        check_vma=False,
    )
```

```python
import functools

import jax
import jax.numpy as jnp
from jax import lax
from jax.experimental import pallas as pl
from jax.experimental.pallas import tpu as pltpu
from jax.sharding import PartitionSpec as P

HQ = 64
KVH = 8
HD = 128
REACH = 3
GRP = 8
STEPS = 2
SMALL = pl.CostEstimate(flops=0, bytes_accessed=0, transcendentals=0)
LITTLE = 1 << 20


def send(value, pairs):
    return lax.ppermute(value, "inst", pairs)


def shift_pairs(count, steps):
    return [(source, (source + steps) % count) for source in range(count)]


def relay_pairs(count):
    first = [(i, i - 3 if i % 4 == 3 else i + 1) for i in range(count)]
    second = [(i, (i + 4) % count if i % 4 == 0 else i) for i in range(count)]
    return first, second


def pack_kernel(cuts, moves_ref, table_ref, pool_ref, *refs):
    outs, sems = refs[:-1], refs[-1]
    copies = []
    for at, (offset, first, some) in enumerate(cuts):
        mover = jnp.int32(0)
        for session in range(1, table_ref.shape[0]):
            mover = jnp.where(moves_ref[session] == offset, jnp.int32(session), mover)
        for page in range(some):
            copies.append(
                pltpu.make_async_copy(
                    pool_ref.at[table_ref[mover, first + page]], outs[at].at[page], sems.at[at, page]
                )
            )
            copies[-1].start()
    for copy in copies:
        copy.wait()


def pack(cuts, moves, page_table, kv_pool):
    shapes = tuple(
        jax.ShapeDtypeStruct((some,) + kv_pool.shape[1:], kv_pool.dtype) for _, _, some in cuts
    )
    most = max(some for _, _, some in cuts)
    return pl.pallas_call(
        functools.partial(pack_kernel, cuts),
        out_shape=shapes,
        in_specs=[
            pl.BlockSpec(memory_space=pltpu.SMEM),
            pl.BlockSpec(memory_space=pltpu.SMEM),
            pl.BlockSpec(memory_space=pltpu.HBM),
        ],
        out_specs=(pl.BlockSpec(memory_space=pl.ANY),) * len(cuts),
        scratch_shapes=[pltpu.SemaphoreType.DMA((len(cuts), most))],
        compiler_params=pltpu.CompilerParams(vmem_limit_bytes=LITTLE),
        cost_estimate=SMALL,
        name="pack",
    )(*(pltpu.with_memory_space_constraint(x, pltpu.HBM) for x in (moves, page_table, kv_pool)))


def place_kernel(rows, guests, *refs):
    pieces, refs = refs[: len(rows)], refs[len(rows) :]
    guest_refs, refs = refs[:guests], refs[guests:]
    if guests:
        out_ref, guest_out_ref, held, sem, guest_sem = refs[-5:]
    else:
        out_ref, sem = refs[-2:]
    copies = []
    for at, (row, piece) in enumerate(zip(rows, pieces)):
        copies.append(
            pltpu.make_async_copy(piece, out_ref.at[pl.ds(row, piece.shape[0])], sem.at[at])
        )
        copies[-1].start()
    if guests:
        one, two = (guest[...] for guest in guest_refs)
        held[...] = jnp.concatenate([one[:1], two[:1], one[1:]], axis=0)
        copies.append(pltpu.make_async_copy(held, guest_out_ref, guest_sem))
        copies[-1].start()
    for copy in copies:
        copy.wait()


def place(pieces, rows, total, buffer=None, guests=()):
    args = (*pieces, *guests)
    aliases = {}
    if buffer is not None:
        aliases = {len(args): 0}
        args += (buffer,)
    shapes = [pltpu.HBM((total,) + pieces[0].shape[1:], pieces[0].dtype)]
    scratch = [pltpu.SemaphoreType.DMA((len(pieces),))]
    if guests:
        guest = (REACH, guests[0].shape[1])
        shapes.append(pltpu.HBM(guest, guests[0].dtype))
        scratch = [pltpu.VMEM(guest, guests[0].dtype)] + scratch + [pltpu.SemaphoreType.DMA]
    return pl.pallas_call(
        functools.partial(place_kernel, rows, len(guests)),
        out_shape=tuple(shapes),
        in_specs=[pl.BlockSpec(memory_space=pl.ANY)] * len(pieces)
        + [pl.BlockSpec(memory_space=pltpu.VMEM)] * len(guests)
        + [pl.BlockSpec(memory_space=pltpu.HBM)] * len(aliases),
        out_specs=(pl.BlockSpec(memory_space=pltpu.HBM),) * len(shapes),
        scratch_shapes=scratch,
        input_output_aliases=aliases,
        compiler_params=pltpu.CompilerParams(vmem_limit_bytes=LITTLE),
        cost_estimate=SMALL,
        name="place",
    )(*args)


def attend_kernel(moves_ref, table_ref, lengths_ref, pool_ref, query_ref, fresh_ref, *refs):
    out_ref, near_ref, far_ref, held, asked, answered, sems = refs
    sessions, pages = table_ref.shape
    span = pages * held.shape[2]
    reads = []
    for session in range(sessions):
        for page in range(pages):
            reads.append(
                pltpu.make_async_copy(
                    pool_ref.at[table_ref[session, page]],
                    held.at[session, page],
                    sems.at[session, page],
                )
            )
            reads[-1].start()
    for head in range(HQ):
        lanes = pl.ds(head * HD, HD)
        for step in range(STEPS):
            asked[head, pl.ds(step * sessions, sessions)] = query_ref[step, :, lanes].astype(
                jnp.float32
            )
    scale = 1.0 / jnp.sqrt(jnp.float32(HD))
    spots = lax.broadcasted_iota(jnp.int32, (1, span), 1)
    for session in range(sessions):
        for page in range(pages):
            reads[session * pages + page].wait()
        visible = spots < lengths_ref[session]
        for head in range(KVH):
            heads = pl.ds(head * GRP, GRP)
            keys = held[session, :, :, pl.ds(head * HD, HD)].reshape(span, HD)
            values = held[session, :, :, pl.ds((KVH + head) * HD, HD)].reshape(span, HD)
            query = jnp.concatenate(
                [asked[heads, step * sessions + session, :] for step in range(STEPS)], axis=0
            )

            def spread(first):
                rows = [
                    fresh_ref[step, :, pl.ds(first, HD)].astype(jnp.float32)[session : session + 1]
                    for step in range(STEPS)
                ]
                return jnp.concatenate([jnp.broadcast_to(row, (GRP, HD)) for row in rows], axis=0)

            scores = lax.dot_general(
                query.astype(jnp.bfloat16),
                keys,
                (((1,), (1,)), ((), ())),
                preferred_element_type=jnp.float32,
            )
            scores = jnp.where(visible, scores * scale, jnp.float32(-1e30))
            own = jnp.sum(query * spread(head * HD), axis=1, keepdims=True) * scale
            highest = jnp.maximum(jnp.max(scores, axis=1, keepdims=True), own)
            expo = jnp.exp(scores - highest)
            own_expo = jnp.exp(own - highest)
            denominator = jnp.sum(expo, axis=1, keepdims=True) + own_expo
            weights = (expo / denominator).astype(jnp.bfloat16)
            own_weight = (own_expo / denominator).astype(jnp.bfloat16).astype(jnp.float32)
            result = jnp.dot(weights, values, preferred_element_type=jnp.float32)
            result = result + own_weight * spread((KVH + head) * HD)
            for step in range(STEPS):
                answered[heads, step * sessions + session, :] = result[
                    step * GRP : (step + 1) * GRP
                ]
    rows = lax.broadcasted_iota(jnp.int32, (sessions, HD), 0)
    distance = jnp.zeros((sessions, HD), jnp.int32)
    for session in range(sessions):
        distance = jnp.where(rows == session, moves_ref[session], distance)
    for head in range(HQ):
        lanes = pl.ds(head * HD, HD)
        first = answered[head, pl.ds(0, sessions)]
        second = answered[head, pl.ds(sessions, sessions)]
        out_ref[0, :, lanes] = first.astype(jnp.bfloat16)
        out_ref[1, :, lanes] = jnp.where(distance > 0, 0.0, second).astype(jnp.bfloat16)
        leaving = [
            jnp.sum(jnp.where(distance == offset, second, 0.0), axis=0, keepdims=True)
            for offset in range(1, REACH + 1)
        ]
        near_ref[:, lanes] = leaving[0].astype(jnp.bfloat16)
        far_ref[:, lanes] = jnp.concatenate(leaving[1:], axis=0).astype(jnp.bfloat16)


def attend(kv_pool, page_table, lengths, moves, query, new_kv):
    sessions, pages = page_table.shape
    shapes = tuple(
        jax.ShapeDtypeStruct(shape, query.dtype)
        for shape in (query.shape, (1, query.shape[2]), (REACH - 1, query.shape[2]))
    )
    return pl.pallas_call(
        attend_kernel,
        out_shape=shapes,
        in_specs=[pl.BlockSpec(memory_space=pltpu.SMEM)] * 3
        + [pl.BlockSpec(memory_space=pltpu.HBM)]
        + [pl.BlockSpec(memory_space=pltpu.VMEM)] * 2,
        out_specs=(pl.BlockSpec(memory_space=pltpu.VMEM),) * len(shapes),
        scratch_shapes=[
            pltpu.VMEM((sessions, pages) + kv_pool.shape[1:], kv_pool.dtype),
            pltpu.VMEM((HQ, STEPS * sessions, HD), jnp.float32),
            pltpu.VMEM((HQ, STEPS * sessions, HD), jnp.float32),
            pltpu.SemaphoreType.DMA((sessions, pages)),
        ],
        compiler_params=pltpu.CompilerParams(vmem_limit_bytes=16 << 20),
        cost_estimate=SMALL,
        name="attend",
    )(
        *(
            pltpu.with_memory_space_constraint(x, pltpu.HBM)
            for x in (moves, page_table, lengths, kv_pool, query, new_kv)
        )
    )


def join_kernel(own_ref, through_ref, out_ref):
    out_ref[...] = jnp.concatenate([own_ref[...], through_ref[1:]], axis=0)


def join(own, through):
    return pl.pallas_call(
        join_kernel,
        out_shape=jax.ShapeDtypeStruct(through.shape, through.dtype),
        in_specs=[pl.BlockSpec(memory_space=pltpu.VMEM)] * 2,
        out_specs=pl.BlockSpec(memory_space=pltpu.VMEM),
        compiler_params=pltpu.CompilerParams(vmem_limit_bytes=LITTLE),
        cost_estimate=SMALL,
        name="join",
    )(own, through)


def body(kv_pool, page_table, lengths, query, new_kv, moves):
    count = lax.axis_size("inst")
    sessions, pages = page_table.shape
    total = REACH * pages
    near, far = pack(((1, 0, pages - 1), (3, 0, pages)), moves, page_table, kv_pool)
    near, far, table, query, new_kv = lax.optimization_barrier(
        (near, far, page_table, query, new_kv)
    )
    rest, middle, late = pack(
        ((1, pages - 1, 1), (2, 0, pages - 1), (2, pages - 1, 1)), moves, table, kv_pool
    )
    near = [near, rest]
    attended, own, ahead = attend(kv_pool, table, lengths, moves, query, new_kv)
    attended, middle, late, own, ahead = lax.optimization_barrier(
        (attended, middle, late, own, ahead)
    )
    if count % 4 == 0:
        hops = relay_pairs(count)
    else:
        hops = (shift_pairs(count, 1),)
    near = [send(part, hops[0]) for part in near]
    far = send(far, shift_pairs(count, 3))
    ahead = send(ahead, shift_pairs(count, 2))
    middle = send(middle, shift_pairs(count, 2))
    (moved,) = place((far,), (2 * pages,), total)
    near, ahead, moved = lax.optimization_barrier((near, ahead, moved))
    rows = join(own, ahead)
    for hop in hops[1:]:
        near = [send(part, hop) for part in near]
    rows = send(rows, shift_pairs(count, 1))
    late = send(late, shift_pairs(count, 2))
    (moved,) = place((middle, *near), (pages, 0, pages - 1), total, moved)
    ahead, moved, late, rows = lax.optimization_barrier((ahead, moved, late, rows))
    moved, guest_attended = place((late,), (2 * pages - 1,), total, moved, (rows, ahead))
    return attended, guest_attended, moved


def solution(mesh):
    return jax.shard_map(
        body,
        mesh=mesh,
        in_specs=(
            P(("group", "inst"), None, None),
            P(("group", "inst"), None),
            P(("group", "inst")),
            P(None, ("group", "inst"), None),
            P(None, ("group", "inst"), None),
            P(("group", "inst")),
        ),
        out_specs=(
            P(None, ("group", "inst"), None),
            P(("group", "inst"), None),
            P(("group", "inst"), None, None),
        ),
        check_vma=False,
    )
```

```python
import functools

import jax
import jax.numpy as jnp
from jax import lax
from jax.experimental import pallas as pl
from jax.experimental.pallas import tpu as pltpu
from jax.sharding import PartitionSpec as P

HQ = 64
KVH = 8
HD = 128
REACH = 3
GRP = 8
STEPS = 2
SMALL = pl.CostEstimate(flops=0, bytes_accessed=0, transcendentals=0)
LITTLE = 1 << 20
LINES = 8
PIECES = 2


def send(value, pairs):
    return lax.ppermute(value, "inst", pairs)


def shift_pairs(count, steps):
    return [(source, (source + steps) % count) for source in range(count)]


def relay_pairs(count):
    first = [(i, i - 3 if i % 4 == 3 else i + 1) for i in range(count)]
    second = [(i, (i + 4) % count if i % 4 == 0 else i) for i in range(count)]
    return first, second


def pack_kernel(cuts, moves_ref, table_ref, pool_ref, *refs):
    outs, sems = refs[:-1], refs[-1]
    copies = []
    for at, (offset, first, some) in enumerate(cuts):
        mover = jnp.int32(0)
        for session in range(1, table_ref.shape[0]):
            mover = jnp.where(moves_ref[session] == offset, jnp.int32(session), mover)
        piece = first
        while piece < first + some:
            span = min(PIECES - piece % PIECES, first + some - piece)
            slot = table_ref[mover, piece // PIECES] * PIECES + piece % PIECES
            copies.append(
                pltpu.make_async_copy(
                    pool_ref.at[pl.ds(slot, span)],
                    outs[at].at[pl.ds(piece - first, span)],
                    sems.at[at, piece // PIECES - first // PIECES],
                )
            )
            copies[-1].start()
            piece += span
    for copy in copies:
        copy.wait()


def pack(cuts, moves, page_table, pool):
    shapes = tuple(jax.ShapeDtypeStruct((some,) + pool.shape[1:], pool.dtype) for _, _, some in cuts)
    return pl.pallas_call(
        functools.partial(pack_kernel, cuts),
        out_shape=shapes,
        in_specs=[
            pl.BlockSpec(memory_space=pltpu.SMEM),
            pl.BlockSpec(memory_space=pltpu.SMEM),
            pl.BlockSpec(memory_space=pltpu.HBM),
        ],
        out_specs=(pl.BlockSpec(memory_space=pl.ANY),) * len(cuts),
        scratch_shapes=[pltpu.SemaphoreType.DMA((len(cuts), page_table.shape[1]))],
        compiler_params=pltpu.CompilerParams(vmem_limit_bytes=LITTLE),
        cost_estimate=SMALL,
        name="pack",
    )(*(pltpu.with_memory_space_constraint(x, pltpu.HBM) for x in (moves, page_table, pool)))


def place_kernel(rows, guests, *refs):
    pieces, refs = refs[: len(rows)], refs[len(rows) :]
    guest_refs, refs = refs[:guests], refs[guests:]
    if guests:
        out_ref, guest_out_ref, held, sem, guest_sem = refs[-5:]
    else:
        out_ref, sem = refs[-2:]
    copies = []
    for at, (row, piece) in enumerate(zip(rows, pieces)):
        copies.append(
            pltpu.make_async_copy(piece, out_ref.at[pl.ds(row, piece.shape[0])], sem.at[at])
        )
        copies[-1].start()
    if guests:
        wide = [guest[...].astype(jnp.float32) for guest in guest_refs]
        for line in range(wide[0].shape[0]):
            lanes = pl.ds(line * wide[0].shape[1], wide[0].shape[1])
            rows = [guest[line : line + 1] for guest in wide]
            held[:, lanes] = jnp.concatenate(rows, axis=0).astype(held.dtype)
        copies.append(pltpu.make_async_copy(held, guest_out_ref, guest_sem))
        copies[-1].start()
    for copy in copies:
        copy.wait()


def place(pieces, rows, total, buffer=None, guests=()):
    args = (*pieces, *guests)
    aliases = {}
    if buffer is not None:
        aliases = {len(args): 0}
        args += (buffer,)
    shapes = [pltpu.HBM((total,) + pieces[0].shape[1:], pieces[0].dtype)]
    scratch = [pltpu.SemaphoreType.DMA((len(pieces),))]
    if guests:
        guest = (REACH, guests[0].size)
        shapes.append(pltpu.HBM(guest, guests[0].dtype))
        scratch = [pltpu.VMEM(guest, guests[0].dtype)] + scratch + [pltpu.SemaphoreType.DMA]
    return pl.pallas_call(
        functools.partial(place_kernel, rows, len(guests)),
        out_shape=tuple(shapes),
        in_specs=[pl.BlockSpec(memory_space=pl.ANY)] * len(pieces)
        + [pl.BlockSpec(memory_space=pltpu.VMEM)] * len(guests)
        + [pl.BlockSpec(memory_space=pltpu.HBM)] * len(aliases),
        out_specs=(pl.BlockSpec(memory_space=pltpu.HBM),) * len(shapes),
        scratch_shapes=scratch,
        input_output_aliases=aliases,
        compiler_params=pltpu.CompilerParams(vmem_limit_bytes=LITTLE),
        cost_estimate=SMALL,
        name="place",
    )(*args)


def attend_kernel(moves_ref, table_ref, lengths_ref, pool_ref, query_ref, fresh_ref, *refs):
    out_ref, guest_refs = refs[0], refs[1 : 1 + REACH]
    held, asked, answered, leaving, sems = refs[1 + REACH :]
    sessions, pages = table_ref.shape
    span = pages * held.shape[2]
    reads = []
    for session in range(sessions):
        for page in range(pages):
            reads.append(
                pltpu.make_async_copy(
                    pool_ref.at[table_ref[session, page]],
                    held.at[session, page],
                    sems.at[session, page],
                )
            )
            reads[-1].start()
    for head in range(HQ):
        lanes = pl.ds(head * HD, HD)
        for step in range(STEPS):
            asked[head, pl.ds(step * sessions, sessions)] = query_ref[step, :, lanes].astype(
                jnp.float32
            )
    scale = 1.0 / jnp.sqrt(jnp.float32(HD))
    spots = lax.broadcasted_iota(jnp.int32, (1, span), 1)
    for session in range(sessions):
        for page in range(pages):
            reads[session * pages + page].wait()
        visible = spots < lengths_ref[session]
        for head in range(KVH):
            heads = pl.ds(head * GRP, GRP)
            keys = held[session, :, :, pl.ds(head * HD, HD)].reshape(span, HD)
            values = held[session, :, :, pl.ds((KVH + head) * HD, HD)].reshape(span, HD)
            query = jnp.concatenate(
                [asked[heads, step * sessions + session, :] for step in range(STEPS)], axis=0
            )

            def spread(first):
                rows = [
                    fresh_ref[step, :, pl.ds(first, HD)].astype(jnp.float32)[session : session + 1]
                    for step in range(STEPS)
                ]
                return jnp.concatenate([jnp.broadcast_to(row, (GRP, HD)) for row in rows], axis=0)

            scores = lax.dot_general(
                query.astype(jnp.bfloat16),
                keys,
                (((1,), (1,)), ((), ())),
                preferred_element_type=jnp.float32,
            )
            scores = jnp.where(visible, scores * scale, jnp.float32(-1e30))
            own = jnp.sum(query * spread(head * HD), axis=1, keepdims=True) * scale
            highest = jnp.maximum(jnp.max(scores, axis=1, keepdims=True), own)
            expo = jnp.exp(scores - highest)
            own_expo = jnp.exp(own - highest)
            denominator = jnp.sum(expo, axis=1, keepdims=True) + own_expo
            weights = (expo / denominator).astype(jnp.bfloat16)
            own_weight = (own_expo / denominator).astype(jnp.bfloat16).astype(jnp.float32)
            result = jnp.dot(weights, values, preferred_element_type=jnp.float32)
            result = result + own_weight * spread((KVH + head) * HD)
            for step in range(STEPS):
                answered[heads, step * sessions + session, :] = result[
                    step * GRP : (step + 1) * GRP
                ]
    rows = lax.broadcasted_iota(jnp.int32, (sessions, HD), 0)
    distance = jnp.zeros((sessions, HD), jnp.int32)
    for session in range(sessions):
        distance = jnp.where(rows == session, moves_ref[session], distance)
    for head in range(HQ):
        lanes = pl.ds(head * HD, HD)
        first = answered[head, pl.ds(0, sessions)]
        second = answered[head, pl.ds(sessions, sessions)]
        out_ref[0, :, lanes] = first.astype(jnp.bfloat16)
        out_ref[1, :, lanes] = jnp.where(distance > 0, 0.0, second).astype(jnp.bfloat16)
        for offset in range(1, REACH + 1):
            row = jnp.sum(jnp.where(distance == offset, second, 0.0), axis=0, keepdims=True)
            leaving[offset - 1, pl.ds(head // LINES, 1), pl.ds(head % LINES * HD, HD)] = row
    for at, guest_ref in enumerate(guest_refs):
        guest_ref[...] = leaving[at].astype(jnp.bfloat16)


def attend(kv_pool, page_table, lengths, moves, query, new_kv):
    sessions, pages = page_table.shape
    shapes = tuple(
        jax.ShapeDtypeStruct(shape, query.dtype)
        for shape in (query.shape,) + ((HQ // LINES, LINES * HD),) * REACH
    )
    return pl.pallas_call(
        attend_kernel,
        out_shape=shapes,
        in_specs=[pl.BlockSpec(memory_space=pltpu.SMEM)] * 3
        + [pl.BlockSpec(memory_space=pltpu.HBM)]
        + [pl.BlockSpec(memory_space=pltpu.VMEM)] * 2,
        out_specs=(pl.BlockSpec(memory_space=pltpu.VMEM),) * len(shapes),
        scratch_shapes=[
            pltpu.VMEM((sessions, pages) + kv_pool.shape[1:], kv_pool.dtype),
            pltpu.VMEM((HQ, STEPS * sessions, HD), jnp.float32),
            pltpu.VMEM((HQ, STEPS * sessions, HD), jnp.float32),
            pltpu.VMEM((REACH, HQ // LINES, LINES * HD), jnp.float32),
            pltpu.SemaphoreType.DMA((sessions, pages)),
        ],
        compiler_params=pltpu.CompilerParams(vmem_limit_bytes=16 << 20),
        cost_estimate=SMALL,
        name="attend",
    )(
        *(
            pltpu.with_memory_space_constraint(x, pltpu.HBM)
            for x in (moves, page_table, lengths, kv_pool, query, new_kv)
        )
    )


def split_kernel(whole_ref, *refs):
    outs, sems = refs[:-1], refs[-1]
    copies, row = [], 0
    for at, out in enumerate(outs):
        copies.append(
            pltpu.make_async_copy(whole_ref.at[pl.ds(row, out.shape[0])], out, sems.at[at])
        )
        copies[-1].start()
        row += out.shape[0]
    for copy in copies:
        copy.wait()


def split(whole, sizes):
    return pl.pallas_call(
        split_kernel,
        out_shape=tuple(
            jax.ShapeDtypeStruct((size,) + whole.shape[1:], whole.dtype) for size in sizes
        ),
        in_specs=[pl.BlockSpec(memory_space=pl.ANY)],
        out_specs=(pl.BlockSpec(memory_space=pl.ANY),) * len(sizes),
        scratch_shapes=[pltpu.SemaphoreType.DMA((len(sizes),))],
        compiler_params=pltpu.CompilerParams(vmem_limit_bytes=LITTLE),
        cost_estimate=SMALL,
        name="split",
    )(whole)


def body(kv_pool, page_table, lengths, query, new_kv, moves):
    count = lax.axis_size("inst")
    sessions, pages = page_table.shape
    each = pages * PIECES
    total = REACH * each
    pool = kv_pool.reshape(-1, kv_pool.shape[1] // PIECES, kv_pool.shape[2])
    near, far = pack(((1, 0, each), (3, 0, each)), moves, page_table, pool)
    near, far, table, query, new_kv = lax.optimization_barrier(
        (near, far, page_table, query, new_kv)
    )
    middle, late = pack(((2, 0, each - 1), (2, each - 1, 1)), moves, table, pool)
    attended, *guests = attend(kv_pool, table, lengths, moves, query, new_kv)
    attended, middle, late, *guests = lax.optimization_barrier((attended, middle, late, *guests))
    if count % 4 == 0:
        hops = relay_pairs(count)
    else:
        hops = (shift_pairs(count, 1),)
    near = send(near, hops[0])
    far = send(far, shift_pairs(count, 3))
    two = send(guests[1], shift_pairs(count, 2))
    three = send(guests[2], shift_pairs(count, 3))
    middle = send(middle, shift_pairs(count, 2))
    (moved,) = place((far,), (2 * each,), total)
    near, two, three, one, moved = lax.optimization_barrier((near, two, three, guests[0], moved))
    near = split(near, (each - 1, 1))
    for hop in hops[1:]:
        near = [send(part, hop) for part in near]
    one = send(one, shift_pairs(count, 1))
    late = send(late, shift_pairs(count, 2))
    (moved,) = place((middle, *near), (each, 0, each - 1), total, moved)
    two, three, moved, late, one = lax.optimization_barrier((two, three, moved, late, one))
    moved, guest_attended = place((late,), (2 * each - 1,), total, moved, (one, two, three))
    return attended, guest_attended, moved.reshape(-1, *kv_pool.shape[1:])


def solution(mesh):
    return jax.shard_map(
        body,
        mesh=mesh,
        in_specs=(
            P(("group", "inst"), None, None),
            P(("group", "inst"), None),
            P(("group", "inst")),
            P(None, ("group", "inst"), None),
            P(None, ("group", "inst"), None),
            P(("group", "inst")),
        ),
        out_specs=(
            P(None, ("group", "inst"), None),
            P(("group", "inst"), None),
            P(("group", "inst"), None, None),
        ),
        check_vma=False,
    )
```

```python
import functools

import jax
import jax.numpy as jnp
from jax import lax
from jax.experimental import pallas as pl
from jax.experimental.pallas import tpu as pltpu
from jax.sharding import PartitionSpec as P

HQ = 64
KVH = 8
HD = 128
REACH = 3
GRP = 8
STEPS = 2
SMALL = pl.CostEstimate(flops=0, bytes_accessed=0, transcendentals=0)
LITTLE = 1 << 20
LINES = 8
PIECES = 4


def send(value, pairs):
    return lax.ppermute(value, "inst", pairs)


def shift_pairs(count, steps):
    return [(source, (source + steps) % count) for source in range(count)]


def relay_pairs(count):
    first = [(i, i - 3 if i % 4 == 3 else i + 1) for i in range(count)]
    second = [(i, (i + 4) % count if i % 4 == 0 else i) for i in range(count)]
    return first, second


def pack_kernel(cuts, moves_ref, table_ref, pool_ref, *refs):
    outs, sems = refs[:-1], refs[-1]
    copies = []
    for at, (offset, first, some) in enumerate(cuts):
        mover = jnp.int32(0)
        for session in range(1, table_ref.shape[0]):
            mover = jnp.where(moves_ref[session] == offset, jnp.int32(session), mover)
        piece = first
        while piece < first + some:
            span = min(PIECES - piece % PIECES, first + some - piece)
            slot = table_ref[mover, piece // PIECES] * PIECES + piece % PIECES
            copies.append(
                pltpu.make_async_copy(
                    pool_ref.at[pl.ds(slot, span)],
                    outs[at].at[pl.ds(piece - first, span)],
                    sems.at[at, piece // PIECES - first // PIECES],
                )
            )
            copies[-1].start()
            piece += span
    for copy in copies:
        copy.wait()


def pack(cuts, moves, page_table, pool):
    shapes = tuple(jax.ShapeDtypeStruct((some,) + pool.shape[1:], pool.dtype) for _, _, some in cuts)
    return pl.pallas_call(
        functools.partial(pack_kernel, cuts),
        out_shape=shapes,
        in_specs=[
            pl.BlockSpec(memory_space=pltpu.SMEM),
            pl.BlockSpec(memory_space=pltpu.SMEM),
            pl.BlockSpec(memory_space=pltpu.HBM),
        ],
        out_specs=(pl.BlockSpec(memory_space=pl.ANY),) * len(cuts),
        scratch_shapes=[pltpu.SemaphoreType.DMA((len(cuts), page_table.shape[1]))],
        compiler_params=pltpu.CompilerParams(vmem_limit_bytes=LITTLE),
        cost_estimate=SMALL,
        name="pack",
    )(*(pltpu.with_memory_space_constraint(x, pltpu.HBM) for x in (moves, page_table, pool)))


def place_kernel(rows, guests, *refs):
    pieces, refs = refs[: len(rows)], refs[len(rows) :]
    guest_refs, refs = refs[:guests], refs[guests:]
    if guests:
        out_ref, guest_out_ref, held, sem, guest_sem = refs[-5:]
    else:
        out_ref, sem = refs[-2:]
    copies = []
    for at, (row, piece) in enumerate(zip(rows, pieces)):
        copies.append(
            pltpu.make_async_copy(piece, out_ref.at[pl.ds(row, piece.shape[0])], sem.at[at])
        )
        copies[-1].start()
    if guests:
        wide = [guest[...].astype(jnp.float32) for guest in guest_refs]
        for line in range(wide[0].shape[0]):
            lanes = pl.ds(line * wide[0].shape[1], wide[0].shape[1])
            rows = [guest[line : line + 1] for guest in wide]
            held[:, lanes] = jnp.concatenate(rows, axis=0).astype(held.dtype)
        copies.append(pltpu.make_async_copy(held, guest_out_ref, guest_sem))
        copies[-1].start()
    for copy in copies:
        copy.wait()


def place(pieces, rows, total, buffer=None, guests=()):
    args = (*pieces, *guests)
    aliases = {}
    if buffer is not None:
        aliases = {len(args): 0}
        args += (buffer,)
    shapes = [pltpu.HBM((total,) + pieces[0].shape[1:], pieces[0].dtype)]
    scratch = [pltpu.SemaphoreType.DMA((len(pieces),))]
    if guests:
        guest = (REACH, guests[0].size)
        shapes.append(pltpu.HBM(guest, guests[0].dtype))
        scratch = [pltpu.VMEM(guest, guests[0].dtype)] + scratch + [pltpu.SemaphoreType.DMA]
    return pl.pallas_call(
        functools.partial(place_kernel, rows, len(guests)),
        out_shape=tuple(shapes),
        in_specs=[pl.BlockSpec(memory_space=pl.ANY)] * len(pieces)
        + [pl.BlockSpec(memory_space=pltpu.VMEM)] * len(guests)
        + [pl.BlockSpec(memory_space=pltpu.HBM)] * len(aliases),
        out_specs=(pl.BlockSpec(memory_space=pltpu.HBM),) * len(shapes),
        scratch_shapes=scratch,
        input_output_aliases=aliases,
        compiler_params=pltpu.CompilerParams(vmem_limit_bytes=LITTLE),
        cost_estimate=SMALL,
        name="place",
    )(*args)


def attend_kernel(moves_ref, table_ref, lengths_ref, pool_ref, query_ref, fresh_ref, *refs):
    out_ref, guest_refs = refs[0], refs[1 : 1 + REACH]
    held, asked, answered, leaving, sems = refs[1 + REACH :]
    sessions, pages = table_ref.shape
    span = pages * held.shape[2]
    reads = []
    for session in range(sessions):
        for page in range(pages):
            reads.append(
                pltpu.make_async_copy(
                    pool_ref.at[table_ref[session, page]],
                    held.at[session, page],
                    sems.at[session, page],
                )
            )
            reads[-1].start()
    for head in range(HQ):
        lanes = pl.ds(head * HD, HD)
        for step in range(STEPS):
            asked[head, pl.ds(step * sessions, sessions)] = query_ref[step, :, lanes].astype(
                jnp.float32
            )
    scale = 1.0 / jnp.sqrt(jnp.float32(HD))
    spots = lax.broadcasted_iota(jnp.int32, (1, span), 1)
    for session in range(sessions):
        for page in range(pages):
            reads[session * pages + page].wait()
        visible = spots < lengths_ref[session]
        for head in range(KVH):
            heads = pl.ds(head * GRP, GRP)
            keys = held[session, :, :, pl.ds(head * HD, HD)].reshape(span, HD)
            values = held[session, :, :, pl.ds((KVH + head) * HD, HD)].reshape(span, HD)
            query = jnp.concatenate(
                [asked[heads, step * sessions + session, :] for step in range(STEPS)], axis=0
            )

            def spread(first):
                rows = [
                    fresh_ref[step, :, pl.ds(first, HD)].astype(jnp.float32)[session : session + 1]
                    for step in range(STEPS)
                ]
                return jnp.concatenate([jnp.broadcast_to(row, (GRP, HD)) for row in rows], axis=0)

            scores = lax.dot_general(
                query.astype(jnp.bfloat16),
                keys,
                (((1,), (1,)), ((), ())),
                preferred_element_type=jnp.float32,
            )
            scores = jnp.where(visible, scores * scale, jnp.float32(-1e30))
            own = jnp.sum(query * spread(head * HD), axis=1, keepdims=True) * scale
            highest = jnp.maximum(jnp.max(scores, axis=1, keepdims=True), own)
            expo = jnp.exp(scores - highest)
            own_expo = jnp.exp(own - highest)
            denominator = jnp.sum(expo, axis=1, keepdims=True) + own_expo
            weights = (expo / denominator).astype(jnp.bfloat16)
            own_weight = (own_expo / denominator).astype(jnp.bfloat16).astype(jnp.float32)
            result = jnp.dot(weights, values, preferred_element_type=jnp.float32)
            result = result + own_weight * spread((KVH + head) * HD)
            for step in range(STEPS):
                answered[heads, step * sessions + session, :] = result[
                    step * GRP : (step + 1) * GRP
                ]
    rows = lax.broadcasted_iota(jnp.int32, (sessions, HD), 0)
    distance = jnp.zeros((sessions, HD), jnp.int32)
    for session in range(sessions):
        distance = jnp.where(rows == session, moves_ref[session], distance)
    for head in range(HQ):
        lanes = pl.ds(head * HD, HD)
        first = answered[head, pl.ds(0, sessions)]
        second = answered[head, pl.ds(sessions, sessions)]
        out_ref[0, :, lanes] = first.astype(jnp.bfloat16)
        out_ref[1, :, lanes] = jnp.where(distance > 0, 0.0, second).astype(jnp.bfloat16)
        for offset in range(1, REACH + 1):
            row = jnp.sum(jnp.where(distance == offset, second, 0.0), axis=0, keepdims=True)
            leaving[offset - 1, pl.ds(head // LINES, 1), pl.ds(head % LINES * HD, HD)] = row
    for at, guest_ref in enumerate(guest_refs):
        guest_ref[...] = leaving[at].astype(jnp.bfloat16)


def attend(kv_pool, page_table, lengths, moves, query, new_kv):
    sessions, pages = page_table.shape
    shapes = tuple(
        jax.ShapeDtypeStruct(shape, query.dtype)
        for shape in (query.shape,) + ((HQ // LINES, LINES * HD),) * REACH
    )
    return pl.pallas_call(
        attend_kernel,
        out_shape=shapes,
        in_specs=[pl.BlockSpec(memory_space=pltpu.SMEM)] * 3
        + [pl.BlockSpec(memory_space=pltpu.HBM)]
        + [pl.BlockSpec(memory_space=pltpu.VMEM)] * 2,
        out_specs=(pl.BlockSpec(memory_space=pltpu.VMEM),) * len(shapes),
        scratch_shapes=[
            pltpu.VMEM((sessions, pages) + kv_pool.shape[1:], kv_pool.dtype),
            pltpu.VMEM((HQ, STEPS * sessions, HD), jnp.float32),
            pltpu.VMEM((HQ, STEPS * sessions, HD), jnp.float32),
            pltpu.VMEM((REACH, HQ // LINES, LINES * HD), jnp.float32),
            pltpu.SemaphoreType.DMA((sessions, pages)),
        ],
        compiler_params=pltpu.CompilerParams(vmem_limit_bytes=16 << 20),
        cost_estimate=SMALL,
        name="attend",
    )(
        *(
            pltpu.with_memory_space_constraint(x, pltpu.HBM)
            for x in (moves, page_table, lengths, kv_pool, query, new_kv)
        )
    )


def split_kernel(whole_ref, *refs):
    outs, sems = refs[:-1], refs[-1]
    copies, row = [], 0
    for at, out in enumerate(outs):
        copies.append(
            pltpu.make_async_copy(whole_ref.at[pl.ds(row, out.shape[0])], out, sems.at[at])
        )
        copies[-1].start()
        row += out.shape[0]
    for copy in copies:
        copy.wait()


def split(whole, sizes):
    return pl.pallas_call(
        split_kernel,
        out_shape=tuple(
            jax.ShapeDtypeStruct((size,) + whole.shape[1:], whole.dtype) for size in sizes
        ),
        in_specs=[pl.BlockSpec(memory_space=pl.ANY)],
        out_specs=(pl.BlockSpec(memory_space=pl.ANY),) * len(sizes),
        scratch_shapes=[pltpu.SemaphoreType.DMA((len(sizes),))],
        compiler_params=pltpu.CompilerParams(vmem_limit_bytes=LITTLE),
        cost_estimate=SMALL,
        name="split",
    )(whole)


def body(kv_pool, page_table, lengths, query, new_kv, moves):
    count = lax.axis_size("inst")
    sessions, pages = page_table.shape
    each = pages * PIECES
    total = REACH * each
    pool = kv_pool.reshape(-1, kv_pool.shape[1] // PIECES, kv_pool.shape[2])
    near, far = pack(((1, 0, each), (3, 0, each)), moves, page_table, pool)
    near, far, table, query, new_kv = lax.optimization_barrier(
        (near, far, page_table, query, new_kv)
    )
    middle, late = pack(((2, 0, each - 1), (2, each - 1, 1)), moves, table, pool)
    attended, *guests = attend(kv_pool, table, lengths, moves, query, new_kv)
    attended, middle, late, *guests = lax.optimization_barrier((attended, middle, late, *guests))
    if count % 4 == 0:
        hops = relay_pairs(count)
    else:
        hops = (shift_pairs(count, 1),)
    near = send(near, hops[0])
    far = send(far, shift_pairs(count, 3))
    two = send(guests[1], shift_pairs(count, 2))
    three = send(guests[2], shift_pairs(count, 3))
    middle = send(middle, shift_pairs(count, 2))
    (moved,) = place((far,), (2 * each,), total)
    near, two, three, one, moved = lax.optimization_barrier((near, two, three, guests[0], moved))
    near = split(near, (each - 1, 1))
    for hop in hops[1:]:
        near = [send(part, hop) for part in near]
    one = send(one, shift_pairs(count, 1))
    late = send(late, shift_pairs(count, 2))
    (moved,) = place((middle, *near), (each, 0, each - 1), total, moved)
    two, three, moved, late, one = lax.optimization_barrier((two, three, moved, late, one))
    moved, guest_attended = place((late,), (2 * each - 1,), total, moved, (one, two, three))
    return attended, guest_attended, moved.reshape(-1, *kv_pool.shape[1:])


def solution(mesh):
    return jax.shard_map(
        body,
        mesh=mesh,
        in_specs=(
            P(("group", "inst"), None, None),
            P(("group", "inst"), None),
            P(("group", "inst")),
            P(None, ("group", "inst"), None),
            P(None, ("group", "inst"), None),
            P(("group", "inst")),
        ),
        out_specs=(
            P(None, ("group", "inst"), None),
            P(("group", "inst"), None),
            P(("group", "inst"), None, None),
        ),
        check_vma=False,
    )
```
